32 devices in a mesh: dp: 8 (over z, y), tensor: 4 (over x, core).
Axes of the slice: x: 2, y: 2, z: 4, core: 2. Of those that a mesh axis runs over, the one named last changes fastest.
Arguments:
- text_states: bfloat16 [8, 256, 4096], P('dp'), may hold values from -6 to 6
- prompt_lengths: int32 [8], P('dp'), may hold values from 1 to 256, as said below
- attn_gain: float32 [4096], replicated, may hold values from 0.1 to 1.9
- query_w: bfloat16 [4096, 2048], P('dp', 'tensor'), may hold values from -0.25 to 0.25
- key_w: bfloat16 [4096, 2048], P('dp', 'tensor'), may hold values from -0.25 to 0.25
- value_w: bfloat16 [4096, 2048], P('dp', 'tensor'), may hold values from -0.09375 to 0.09375
- out_w: bfloat16 [2048, 4096], P('tensor', 'dp'), may hold values from -0.125 to 0.125
- context_w: bfloat16 [4096, 2432], P('tensor', 'dp'), may hold values from -0.09375 to 0.09375
- mod_scale: float32 [8, 2432], P('dp'), may hold values from -0.5 to 0.5
- mod_shift: float32 [8, 2432], P('dp'), may hold values from -5 to 5
- text_key_w: bfloat16 [2432, 1536], P('dp', 'tensor'), may hold values from -0.125 to 0.125
- text_value_w: bfloat16 [2432, 1536], P('dp', 'tensor'), may hold values from -0.125 to 0.125
- image_query: bfloat16 [8, 512, 1536], P('dp', 'tensor'), may hold values from -30 to 30
- image_key: bfloat16 [8, 512, 1536], P('dp', 'tensor'), may hold values from -30 to 30
- image_value: bfloat16 [8, 512, 1536], P('dp', 'tensor'), may hold values from -6 to 6
Outputs:
- image_mixed: bfloat16 [8, 512, 1536], P('dp', 'tensor')
The draws below stay inside these ranges and needn't reach their ends.
Inputs may be any that keep to these rules, and one draw needn't show every extreme that they name: `prompt_lengths`: some prompt has all 256 tokens in every draw.
All inputs are finite; a program needn't handle non-finite values.
Results may differ from the reference program's by a relative error of at most 0.015.
Values may be sent and summed in bfloat16 or wider, within the bound.
A program may use at most 64 MiB of HBM per device.

```python
import math
import jax
import jax.numpy as jnp
from jax import lax

ENC = 4096
ENC_HEADS = 32
HEAD = 64
WIDTH = 2432
HEADS = 24
SLOTS = 256
LAT = 512
SAMPLES = 8
N_TENSOR = 4


def shared_normal(key, shape, limit):
    return jnp.clip(jax.random.normal(key, shape, jnp.float32), -limit, limit)


def draw_query_w(key, part):
    key = jax.random.fold_in(key, 11)
    own = 0.35 * shared_normal(key, (ENC, ENC_HEADS * HEAD), 6.0)
    return jnp.clip(own / math.sqrt(ENC), -0.25, 0.25).astype(jnp.bfloat16)


def draw_key_w(key, part):
    key = jax.random.fold_in(key, 12)
    own = 0.35 * shared_normal(key, (ENC, ENC_HEADS * HEAD), 6.0)
    return jnp.clip(own / math.sqrt(ENC), -0.25, 0.25).astype(jnp.bfloat16)


def draw_image_query(key, part):
    key = jax.random.fold_in(key, 21)
    own = shared_normal(key, (SAMPLES, LAT, HEADS * HEAD), 6.0)
    return own.astype(jnp.bfloat16)


def draw_image_key(key, part):
    key = jax.random.fold_in(key, 22)
    own = shared_normal(key, (SAMPLES, LAT, HEADS * HEAD), 6.0)
    return own.astype(jnp.bfloat16)


def draw_prompt_lengths(key, part):
    key = jax.random.fold_in(key, 31)
    first, second = jax.random.split(key)
    lengths = jax.random.randint(first, (SAMPLES,), 1, SLOTS + 1, jnp.int32)
    where = jax.random.randint(second, (), 0, SAMPLES, jnp.int32)
    return lengths.at[where].set(SLOTS)


def block_levels(rng, dims, shards, smallest, top_value):
    loudness = 1.0
    for position, parts in shards:
        draws = jax.random.uniform(jax.random.fold_in(jax.random.fold_in(rng, 6), position), (parts,), jnp.float32, smallest / len(shards), top_value / len(shards))
        loudness = loudness * jnp.repeat(jnp.exp(draws), dims[position] // parts).reshape((-1,) + (1,) * (len(dims) - 1 - position))
    return loudness


def centred(own_key, extent, scale, bound, cuts=(), dtype=jnp.bfloat16):
    array = scale * jax.random.normal(own_key, extent, jnp.float32)
    if cuts:
        array = array * block_levels(own_key, extent, cuts, -0.22, 0.18)
    return jnp.clip(array, -bound, bound).astype(dtype)


def setup_inputs(seed: int = 0) -> dict:
    splits = jax.random.split(jax.random.key(seed), 16)
    return {
        "text_states": centred(splits[0], (SAMPLES, SLOTS, ENC), 1.0, 6.0, ((0, 8),)),
        "prompt_lengths": draw_prompt_lengths(jax.random.fold_in(splits[15], 71), 0),
        "attn_gain": jnp.clip(1.0 + 0.18 * jax.random.normal(splits[2], (ENC,), jnp.float32), 0.1, 1.9),
        "query_w": draw_query_w(jax.random.fold_in(splits[15], 71), 0),
        "key_w": draw_key_w(jax.random.fold_in(splits[15], 71), 0),
        "value_w": centred(splits[5], (ENC, ENC_HEADS * HEAD), ENC ** -0.5, 0.09375, ((0, 8), (1, 4))),
        "out_w": centred(splits[6], (ENC_HEADS * HEAD, ENC), (ENC_HEADS * HEAD) ** -0.5, 0.125, ((0, 4), (1, 8))),
        "context_w": centred(splits[7], (ENC, WIDTH), ENC ** -0.5, 0.09375, ((0, 4), (1, 8))),
        "mod_scale": jnp.clip(jax.random.uniform(splits[8], (SAMPLES, WIDTH), jnp.float32, -0.5, 0.5) * block_levels(splits[8], (SAMPLES, WIDTH), ((0, 8),), -0.4, 0.0), -0.5, 0.5),
        "mod_shift": centred(splits[9], (SAMPLES, WIDTH), 1.0, 5.0, ((0, 8),), jnp.float32),
        "text_key_w": centred(splits[10], (WIDTH, HEADS * HEAD), WIDTH ** -0.5, 0.125, ((0, 8), (1, 4))),
        "text_value_w": centred(splits[11], (WIDTH, HEADS * HEAD), WIDTH ** -0.5, 0.125, ((0, 8), (1, 4))),
        "image_query": draw_image_query(jax.random.fold_in(splits[15], 71), 0),
        "image_key": draw_image_key(jax.random.fold_in(splits[15], 71), 0),
        "image_value": centred(splits[14], (SAMPLES, LAT, HEADS * HEAD), 1.0, 6.0, ((0, 8), (1, 4))),
    }


EPS = 1e-06

def rms_scale(values, gain):
    return values * lax.rsqrt(lax.optimization_barrier(jnp.mean(values * values, axis=-1, keepdims=True)) + EPS) * gain

def masked_softmax(scores, valid):
    scores = jnp.where(valid, scores, -jnp.inf)
    top = lax.optimization_barrier(jnp.max(scores, axis=-1, keepdims=True))
    expo = jnp.exp(scores - top)
    return (expo, lax.optimization_barrier(jnp.sum(expo, axis=-1, keepdims=True)))

def rounded_sum(partial_value):
    rounded = lax.optimization_barrier(partial_value.astype(jnp.bfloat16))
    return lax.optimization_barrier(jnp.sum(rounded.astype(jnp.float32), axis=0))

def reference(text_states, prompt_lengths, attn_gain, query_w, key_w, value_w, out_w, context_w, mod_scale, mod_shift, text_key_w, text_value_w, image_query, image_key, image_value):
    enc_block = ENC_HEADS * HEAD // N_TENSOR
    feature_block = ENC // N_TENSOR
    out_blocks = out_w.astype(jnp.float32).reshape(N_TENSOR, enc_block, ENC)
    context_blocks = context_w.astype(jnp.float32).reshape(N_TENSOR, feature_block, WIDTH)

    def one_sample(items):
        text_row, length, scale_row, shift_row, query_row, key_row, value_row = items
        states = text_row.astype(jnp.float32)
        normed = rms_scale(states, attn_gain).astype(jnp.bfloat16)

        def project(weight):
            product = jnp.dot(normed, weight, preferred_element_type=jnp.float32)
            return product.astype(jnp.bfloat16).reshape(SLOTS, ENC_HEADS, HEAD)
        enc_q = project(query_w)
        enc_k = project(key_w)
        enc_v = project(value_w)
        scores = jnp.einsum('qhd,khd->hqk', enc_q.astype(jnp.float32), enc_k.astype(jnp.float32))
        valid = (lax.iota(jnp.int32, SLOTS) < length)[None, None, :]
        expo, total = masked_softmax(scores, valid)
        mixed = jnp.einsum('hqk,khd->qhd', expo.astype(jnp.bfloat16).astype(jnp.float32), enc_v.astype(jnp.float32))
        mixed = (mixed / jnp.transpose(total, (1, 0, 2))).astype(jnp.bfloat16)
        grouped = mixed.reshape(SLOTS, N_TENSOR, enc_block).astype(jnp.float32)
        attn = rounded_sum(jnp.einsum('snb,nbe->nse', grouped, out_blocks))
        embedded = (states + attn).astype(jnp.bfloat16)
        pieces = embedded.reshape(SLOTS, N_TENSOR, feature_block).astype(jnp.float32)
        context = rounded_sum(jnp.einsum('snb,nbw->nsw', pieces, context_blocks))
        centered = context - lax.optimization_barrier(jnp.mean(context, axis=-1, keepdims=True))
        spread = lax.optimization_barrier(jnp.mean(centered * centered, axis=-1, keepdims=True))
        modulated = (centered * lax.rsqrt(spread + EPS) * (1.0 + scale_row) + shift_row).astype(jnp.bfloat16)
        text_k = jnp.dot(modulated, text_key_w, preferred_element_type=jnp.float32).astype(jnp.bfloat16)
        text_v = jnp.dot(modulated, text_value_w, preferred_element_type=jnp.float32).astype(jnp.bfloat16)
        all_keys = jnp.concatenate([key_row, text_k], axis=0).reshape(LAT + SLOTS, HEADS, HEAD)
        all_values = jnp.concatenate([value_row, text_v], axis=0).reshape(LAT + SLOTS, HEADS, HEAD)
        queries = query_row.reshape(LAT, HEADS, HEAD)
        joint = jnp.einsum('qhd,khd->hqk', queries.astype(jnp.float32), all_keys.astype(jnp.float32)) * HEAD ** (-0.5)
        slot_ok = jnp.concatenate([lax.iota(jnp.int32, LAT) >= 0, lax.iota(jnp.int32, SLOTS) < length])
        joint_exp, joint_total = masked_softmax(joint, slot_ok[None, None, :])
        result = jnp.einsum('hqk,khd->qhd', joint_exp.astype(jnp.bfloat16).astype(jnp.float32), all_values.astype(jnp.float32))
        result = result / jnp.transpose(joint_total, (1, 0, 2))
        return result.astype(jnp.bfloat16).reshape(LAT, HEADS * HEAD)
    return lax.map(one_sample, (text_states, prompt_lengths, mod_scale, mod_shift, image_query, image_key, image_value))
```

```python
import functools

import jax
import jax.numpy as jnp
from jax import lax
from jax.experimental import pallas as pl
from jax.experimental.pallas import tpu as pltpu
from jax.sharding import PartitionSpec as P

HEAD = 64
EPS = 1e-06
MESH = pl.DeviceIdType.MESH
F32 = jnp.float32
BF16 = jnp.bfloat16


def split_rows(rows, count):
    if rows % 16:
        return [(0, rows)]
    size = -(-rows // (count * 16)) * 16
    return [(i * size, min(size, rows - i * size)) for i in range(count)]


def kernel(n, nt, *refs):
    (
        len_ref, x_ref, gain_ref, scale_ref, shift_ref,
        q_in, k_in, v_in, o_in, c_in, tk_in, tv_in, iq_in, ik_in, iv_in,
        out_ref,
        wq, wk, wv, wo, wc, wtk, wtv,
        normed, eq, ek, ev, mixed, part, part_in, emb, ctx, ctx_in, mod,
        iq, ik, iv, tk, tv, att,
        own_sem, ring_send, ring_recv, img_send, img_recv, img_own,
        part_send, part_recv, ctx_send, ctx_recv, mod_send, mod_recv,
        att_send, att_recv, att_own,
    ) = refs
    d = lax.axis_index("dp")
    t = lax.axis_index("tensor")
    half = n // 2

    def device_at(place):
        back = place // half
        return 2 * (place * (1 - back) + (n - 1 - place) * back) + back

    odd = d % 2
    place = (d // 2) * (1 - odd) + (n - 1 - d // 2) * odd
    right = device_at((place + 1) % n)
    left = device_at((place + n - 1) % n)
    peers = [(t + k) % nt for k in range(1, nt)]

    barrier = pltpu.get_barrier_semaphore()
    for neighbour in (left, right):
        pl.semaphore_signal(barrier, inc=1, device_id=(neighbour, t), device_id_type=MESH)
    for peer in peers:
        pl.semaphore_signal(barrier, inc=1, device_id=(d, peer), device_id_type=MESH)

    weights = [(q_in, wq), (k_in, wk), (v_in, wv), (o_in, wo), (c_in, wc), (tk_in, wtk), (tv_in, wtv)]
    own = [
        pltpu.make_async_copy(src, dst.at[d], own_sem.at[i])
        for i, (src, dst) in enumerate(weights)
    ]
    for copy in own:
        copy.start()
    pl.semaphore_wait(barrier, 2 + nt - 1)

    chunks = []

    def add(weight, index, runs, forward):
        made = []
        for run in runs:
            made.append((len(chunks), weight, run, forward))
            chunks.append(made[-1])
        return made

    def hop(chunk, step, incoming=False):
        number, weight, (start, size), forward = chunk
        back = step + 1 if incoming else step
        owner = device_at((place - back + n) % n if forward else (place + back) % n)
        view = weight.at[owner, pl.ds(start, size)] if size < weight.shape[1] else weight.at[owner]
        return pltpu.make_async_remote_copy(
            src_ref=view, dst_ref=view,
            send_sem=ring_send.at[number], recv_sem=ring_recv.at[number, step],
            device_id=(right if forward else left, t), device_id_type=MESH,
        )

    def open_ring(group):
        for chunk in group:
            hop(chunk, 0).start()

    def run_ring(group, first, last):
        @pl.loop(first, last)
        def _(step):
            for chunk in group:
                hop(chunk, step - 1, incoming=True).wait_recv()
                hop(chunk, step - 1).wait_send()
                hop(chunk, step).start()

    def close_ring(group):
        for chunk in group:
            hop(chunk, n - 2, incoming=True).wait_recv()
            hop(chunk, n - 2).wait_send()

    rows = q_in.shape[0]
    group_qk = add(wq, 0, split_rows(rows, 2), True) + add(wk, 1, split_rows(rows, 2), False)
    group_vo = add(wv, 2, split_rows(rows, 2), True) + add(wo, 3, split_rows(o_in.shape[0], 2), False)
    quarters = split_rows(c_in.shape[0], 4)
    group_c = add(wc, 4, quarters[:2], True) + add(wc, 4, quarters[2:], False)
    trows = tk_in.shape[0]
    group_t = add(wtk, 5, split_rows(trows, 2), True) + add(wtv, 6, split_rows(trows, 2), False)

    own[0].wait()
    own[1].wait()
    open_ring(group_qk)

    lat, cols = iq.shape[1:]

    def columns_of(ref, who):
        if len(ref.shape) == 3:
            return ref.at[who]
        return ref.at[:, pl.ds(pl.multiple_of(who * cols, 128), cols)]

    def image_copy(a, src, dst, peer, place_of):
        return pltpu.make_async_remote_copy(
            src_ref=columns_of(src, peer),
            dst_ref=dst.at[place_of],
            send_sem=img_send.at[a, peer], recv_sem=img_recv.at[a, place_of],
            device_id=(d, peer), device_id_type=MESH,
        )

    images = [(iq_in, iq), (ik_in, ik), (iv_in, iv)]
    image_own = []
    for a, (src, dst) in enumerate(images):
        copy = pltpu.make_async_copy(
            columns_of(src, t), dst.at[t], img_own.at[a]
        )
        copy.start()
        image_own.append(copy)
        for peer in peers:
            image_copy(a, src, dst, peer, t).start()

    for copy in own[2:]:
        copy.wait()

    slots, enc = x_ref.shape
    length = len_ref[0]

    @pl.loop(0, slots // 32)
    def _(i):
        block = pl.ds(pl.multiple_of(i * 32, 32), 32)
        x = x_ref[block, :].astype(F32)
        scale = lax.rsqrt(jnp.mean(x * x, axis=-1, keepdims=True) + EPS)
        normed[block, :] = (x * scale * gain_ref[...]).astype(BF16)

    width = q_in.shape[1]

    def project(weight, result):
        @pl.loop(0, width // 256)
        def _(j):
            block = pl.ds(pl.multiple_of(j * 256, 256), 256)
            w = weight[:, :, block].reshape(enc, 256)
            result[:, block] = jnp.dot(normed[...], w, preferred_element_type=F32).astype(BF16)

    run_ring(group_qk, 1, n - 1)
    open_ring(group_vo)
    close_ring(group_qk)
    project(wq, eq)
    project(wk, ek)

    run_ring(group_vo, 1, n - 1)
    open_ring(group_c)
    open_ring(group_t)
    close_ring(group_vo)
    project(wv, ev)

    for h in range(width // HEAD):
        at = slice(h * HEAD, (h + 1) * HEAD)
        scores = lax.dot_general(
            eq[:, at], ek[:, at], (((1,), (1,)), ((), ())), preferred_element_type=F32
        )
        valid = lax.broadcasted_iota(jnp.int32, scores.shape, 1) < length
        scores = jnp.where(valid, scores, -jnp.inf)
        expo = jnp.exp(scores - jnp.max(scores, axis=-1, keepdims=True))
        total = jnp.sum(expo, axis=-1, keepdims=True)
        value = jnp.dot(expo.astype(BF16), ev[:, at], preferred_element_type=F32)
        mixed[:, at] = (value / total).astype(BF16)

    ocols = o_in.shape[1]
    share = enc // nt
    per = share // ocols

    @pl.loop(0, n)
    def _(j):
        value = jnp.dot(mixed[...], wo[j], preferred_element_type=F32).astype(BF16)
        part[j // per, :, pl.ds(pl.multiple_of((j % per) * ocols, 128), ocols)] = value

    def part_copy(peer, place_of):
        return pltpu.make_async_remote_copy(
            src_ref=part.at[peer], dst_ref=part_in.at[place_of],
            send_sem=part_send.at[peer], recv_sem=part_recv.at[place_of],
            device_id=(d, peer), device_id_type=MESH,
        )

    for peer in peers:
        part_copy(peer, t).start()
    run_ring(group_c, 1, n - 1)
    for peer in peers:
        part_copy(peer, peer).wait_recv()

    @pl.loop(0, slots // 32)
    def _(i):
        block = pl.ds(pl.multiple_of(i * 32, 32), 32)
        total = part[t, block, :].astype(F32)
        for peer in peers:
            total = total + part_in[peer, block, :].astype(F32)
        x = x_ref[block, pl.ds(pl.multiple_of(t * share, 128), share)].astype(F32)
        emb[block, :] = (x + total).astype(BF16)

    close_ring(group_c)

    @pl.loop(0, n)
    def _(j):
        ctx[j] = jnp.dot(emb[...], wc[j], preferred_element_type=F32).astype(BF16)

    trow = slots // nt

    def token_rows(who):
        return pl.ds(pl.multiple_of(who * trow, 16), trow)

    def ctx_copy(peer, place_of):
        return pltpu.make_async_remote_copy(
            src_ref=ctx.at[:, token_rows(peer)], dst_ref=ctx_in.at[place_of],
            send_sem=ctx_send.at[peer], recv_sem=ctx_recv.at[place_of],
            device_id=(d, peer), device_id_type=MESH,
        )

    for peer in peers:
        ctx_copy(peer, t).start()
    middle = 1 + (n - 1) // 3
    run_ring(group_t, 1, middle)
    for peer in peers:
        ctx_copy(peer, peer).wait_recv()
    context = ctx[:, token_rows(t), :].astype(F32)
    for peer in peers:
        context = context + ctx_in[peer].astype(F32)
    features = context.shape[0] * context.shape[2]

    def mean(values):
        return jnp.sum(jnp.sum(values, axis=0), axis=-1, keepdims=True)[None] / features

    centered = context - mean(context)
    spread = mean(centered * centered)
    modulated = centered * lax.rsqrt(spread + EPS) * (1.0 + scale_ref[...]) + shift_ref[...]
    mod[:, token_rows(t), :] = modulated.astype(BF16)

    def mod_copy(peer, place_of):
        view = mod.at[:, token_rows(place_of)]
        return pltpu.make_async_remote_copy(
            src_ref=view, dst_ref=view,
            send_sem=mod_send.at[peer], recv_sem=mod_recv.at[place_of],
            device_id=(d, peer), device_id_type=MESH,
        )

    for peer in peers:
        mod_copy(peer, t).start()
    run_ring(group_t, middle, n - 1)
    for a, (src, dst) in enumerate(images):
        image_own[a].wait()
        for peer in peers:
            image_copy(a, src, dst, peer, peer).wait_recv()
    for peer in peers:
        mod_copy(peer, peer).wait_recv()
    close_ring(group_t)

    def text_project(weight, result):
        total = jnp.dot(mod[0], weight[0], preferred_element_type=F32)
        for j in range(1, n):
            total = total + jnp.dot(mod[j], weight[j], preferred_element_type=F32)
        result[...] = total.astype(BF16)

    text_project(wtk, tk)
    text_project(wtv, tv)

    for h in range(cols // HEAD):
        at = slice(h * HEAD, (h + 1) * HEAD)
        keys = ik[:, :, at].reshape(nt * lat, HEAD)
        values = iv[:, :, at].reshape(nt * lat, HEAD)
        queries = iq[:, :, at].reshape(nt * lat, HEAD)
        score = functools.partial(
            lax.dot_general, dimension_numbers=(((1,), (1,)), ((), ())), preferred_element_type=F32
        )
        first = score(queries, keys) * HEAD ** (-0.5)
        second = score(queries, tk[:, at]) * HEAD ** (-0.5)
        valid = lax.broadcasted_iota(jnp.int32, second.shape, 1) < length
        second = jnp.where(valid, second, -jnp.inf)
        top = jnp.maximum(
            jnp.max(first, axis=-1, keepdims=True), jnp.max(second, axis=-1, keepdims=True)
        )
        first = jnp.exp(first - top)
        second = jnp.exp(second - top)
        total = jnp.sum(first, axis=-1, keepdims=True) + jnp.sum(second, axis=-1, keepdims=True)
        value = jnp.dot(first.astype(BF16), values, preferred_element_type=F32)
        value = value + jnp.dot(second.astype(BF16), tv[:, at], preferred_element_type=F32)
        att[:, :, at] = (value / total).astype(BF16).reshape(nt, lat, HEAD)

    def att_copy(peer, place_of):
        return pltpu.make_async_remote_copy(
            src_ref=att.at[peer], dst_ref=columns_of(out_ref, place_of),
            send_sem=att_send.at[peer], recv_sem=att_recv.at[place_of],
            device_id=(d, peer), device_id_type=MESH,
        )

    for peer in peers:
        att_copy(peer, t).start()
    copy = pltpu.make_async_copy(att.at[t], columns_of(out_ref, t), att_own)
    copy.start()
    copy.wait()
    for peer in peers:
        for a, (src, dst) in enumerate(images):
            image_copy(a, src, dst, peer, t).wait_send()
        part_copy(peer, t).wait_send()
        ctx_copy(peer, t).wait_send()
        mod_copy(peer, t).wait_send()
        att_copy(peer, t).wait_send()
    for peer in peers:
        att_copy(peer, peer).wait_recv()


def per_device(
    n, nt,
    text_states, prompt_lengths, attn_gain, query_w, key_w, value_w, out_w, context_w,
    mod_scale, mod_shift, text_key_w, text_value_w, image_query, image_key, image_value,
):
    prompts, slots, enc = text_states.shape
    lat, joint = image_query.shape[1:]
    width = query_w.shape[1]
    cols = joint // nt
    ccols = context_w.shape[1]
    vmem = pl.BlockSpec(memory_space=pltpu.VMEM)
    anywhere = pl.BlockSpec(memory_space=pl.ANY)
    dma = pltpu.SemaphoreType.DMA
    scratch = [pltpu.VMEM((n,) + w.shape, BF16) for w in (query_w, key_w, value_w, out_w, context_w, text_key_w, text_value_w)]
    scratch += [
        pltpu.VMEM((slots, enc), BF16),
        pltpu.VMEM((slots, width), BF16),
        pltpu.VMEM((slots, width), BF16),
        pltpu.VMEM((slots, width), BF16),
        pltpu.VMEM((slots, width), BF16),
        pltpu.VMEM((nt, slots, enc // nt), BF16),
        pltpu.VMEM((nt, slots, enc // nt), BF16),
        pltpu.VMEM((slots, enc // nt), BF16),
        pltpu.VMEM((n, slots, ccols), BF16),
        pltpu.VMEM((nt, n, slots // nt, ccols), BF16),
        pltpu.VMEM((n, slots, ccols), BF16),
        pltpu.VMEM((nt, lat, cols), BF16),
        pltpu.VMEM((nt, lat, cols), BF16),
        pltpu.VMEM((nt, lat, cols), BF16),
        pltpu.VMEM((slots, cols), BF16),
        pltpu.VMEM((slots, cols), BF16),
        pltpu.VMEM((nt, lat, cols), BF16),
        dma((7,)), dma((16,)), dma((16, n - 1)),
        dma((3, nt)), dma((3, nt)), dma((3,)),
        dma((nt,)), dma((nt,)), dma((nt,)), dma((nt,)), dma((nt,)), dma((nt,)),
        dma((nt,)), dma((nt,)), dma,
    ]
    flops = 2 * slots * (enc * width * 4 + enc // nt * ccols * n + ccols * n * cols * 2) + 4 * lat * nt * (lat * nt + slots) * cols
    apart = cols % 128 != 0

    def laid_out(array):
        array = array.reshape(lat, joint)
        return array.reshape(lat, nt, cols).swapaxes(0, 1) if apart else array

    result = pl.pallas_call(
        functools.partial(kernel, n, nt),
        out_shape=jax.ShapeDtypeStruct((nt, lat, cols) if apart else (lat, joint), BF16),
        in_specs=[pl.BlockSpec(memory_space=pltpu.SMEM)] + [vmem] * 4 + [anywhere] * 10,
        out_specs=vmem,
        scratch_shapes=scratch,
        compiler_params=pltpu.CompilerParams(
            collective_id=0, has_side_effects=True, vmem_limit_bytes=60 * 2**20
        ),
        cost_estimate=pl.CostEstimate(flops=flops, bytes_accessed=12 * 2**20, transcendentals=3 * 2**20),
    )(
        prompt_lengths,
        text_states.reshape(slots, enc),
        attn_gain.reshape(1, enc),
        mod_scale.reshape(n, 1, ccols),
        mod_shift.reshape(n, 1, ccols),
        query_w, key_w, value_w, out_w, context_w, text_key_w, text_value_w,
        laid_out(image_query), laid_out(image_key), laid_out(image_value),
    )
    if apart:
        result = result.swapaxes(0, 1)
    return result.reshape(1, lat, joint)


def solution(mesh):
    n, nt = mesh.shape["dp"], mesh.shape["tensor"]
    in_specs = (
        P("dp", None, None),
        P("dp"),
        P(),
        P("dp", "tensor"),
        P("dp", "tensor"),
        P("dp", "tensor"),
        P("tensor", "dp"),
        P("tensor", "dp"),
        P("dp", None),
        P("dp", None),
        P("dp", "tensor"),
        P("dp", "tensor"),
        P("dp", "tensor", None),
        P("dp", "tensor", None),
        P("dp", "tensor", None),
    )
    return jax.shard_map(
        functools.partial(per_device, n, nt),
        mesh=mesh, in_specs=in_specs, out_specs=P("dp", "tensor", None), check_vma=False,
    )
```

```python
import functools

import jax
import jax.numpy as jnp
from jax import lax
from jax.experimental import pallas as pl
from jax.experimental.pallas import tpu as pltpu
from jax.sharding import PartitionSpec as P

HEAD = 64
EPS = 1e-06
MESH = pl.DeviceIdType.MESH
F32 = jnp.float32
BF16 = jnp.bfloat16


def split_rows(rows, count):
    if rows % 16:
        return [(0, rows)]
    size = -(-rows // (count * 16)) * 16
    return [(i * size, min(size, rows - i * size)) for i in range(count)]


def kernel(n, nt, *refs):
    (
        len_ref, x_ref, gain_ref, scale_ref, shift_ref,
        q_in, k_in, v_in, o_in, c_in, tk_in, tv_in, iq_in, ik_in, iv_in,
        out_ref,
        wq, wk, wv, wo, wc, wtk, wtv,
        normed, eq, ek, ev, mixed, part, part_in, emb, ctx, ctx_in, mod,
        iq, ik, iv, tk, tv, att, scale, shift, probs, sums, part_top, part_sum, part_out,
        own_sem, ring_send, ring_recv, img_send, img_recv, img_own,
        part_send, part_recv, ctx_send, ctx_recv, mod_send, mod_recv,
        att_send, att_recv, att_own,
    ) = refs
    d = lax.axis_index("dp")
    t = lax.axis_index("tensor")
    half = n // 2

    def device_at(place):
        back = place // half
        return 2 * (place * (1 - back) + (n - 1 - place) * back) + back

    odd = d % 2
    place = (d // 2) * (1 - odd) + (n - 1 - d // 2) * odd
    right = device_at((place + 1) % n)
    left = device_at((place + n - 1) % n)
    peers = [(t + k) % nt for k in range(1, nt)]

    barrier = pltpu.get_barrier_semaphore()
    for neighbour in (left, right):
        pl.semaphore_signal(barrier, inc=1, device_id=(neighbour, t), device_id_type=MESH)
    for peer in peers:
        pl.semaphore_signal(barrier, inc=1, device_id=(d, peer), device_id_type=MESH)

    weights = [(q_in, wq), (k_in, wk), (v_in, wv), (o_in, wo), (c_in, wc), (tk_in, wtk), (tv_in, wtv)]
    own = [
        pltpu.make_async_copy(src, dst.at[d], own_sem.at[i])
        for i, (src, dst) in enumerate(weights)
    ]
    for copy in own:
        copy.start()
    pl.semaphore_wait(barrier, 2 + nt - 1)

    chunks = []

    def add(weight, index, runs, forward):
        made = []
        for run in runs:
            made.append((len(chunks), weight, run, forward))
            chunks.append(made[-1])
        return made

    def hop(chunk, step, incoming=False):
        number, weight, (start, size), forward = chunk
        back = step + 1 if incoming else step
        owner = device_at((place - back + n) % n if forward else (place + back) % n)
        view = weight.at[owner, pl.ds(start, size)] if size < weight.shape[1] else weight.at[owner]
        return pltpu.make_async_remote_copy(
            src_ref=view, dst_ref=view,
            send_sem=ring_send.at[number], recv_sem=ring_recv.at[number, step],
            device_id=(right if forward else left, t), device_id_type=MESH,
        )

    def open_ring(group):
        for chunk in group:
            hop(chunk, 0).start()

    def move(group, step):
        for chunk in group:
            hop(chunk, step - 1, incoming=True).wait_recv()
            hop(chunk, step - 1).wait_send()
            hop(chunk, step).start()

    def run_ring(group, first, last, tasks=()):
        tasks = list(tasks)[: max(last - first, 0)]
        for i, task in enumerate(tasks):
            move(group, first + i)
            task()

        @pl.loop(first + len(tasks), last)
        def _(step):
            move(group, step)

    def close_ring(group):
        for chunk in group:
            hop(chunk, n - 2, incoming=True).wait_recv()
            hop(chunk, n - 2).wait_send()

    rows = q_in.shape[0]
    group_qk = add(wq, 0, split_rows(rows, 2), True) + add(wk, 1, split_rows(rows, 2), False)
    group_vo = add(wv, 2, split_rows(rows, 2), True) + add(wo, 3, split_rows(o_in.shape[0], 2), False)
    quarters = split_rows(c_in.shape[0], 4)
    group_c = add(wc, 4, quarters[:2], True) + add(wc, 4, quarters[2:], False)
    trows = tk_in.shape[0]
    group_t = add(wtk, 5, split_rows(trows, 2), True) + add(wtv, 6, split_rows(trows, 2), False)

    own[0].wait()
    own[1].wait()
    open_ring(group_qk)

    lat, cols = iq.shape[1:]

    def columns_of(ref, who):
        if len(ref.shape) == 3:
            return ref.at[who]
        return ref.at[:, pl.ds(pl.multiple_of(who * cols, 128), cols)]

    def image_copy(a, src, dst, peer, place_of):
        return pltpu.make_async_remote_copy(
            src_ref=columns_of(src, peer),
            dst_ref=dst.at[place_of],
            send_sem=img_send.at[a, peer], recv_sem=img_recv.at[a, place_of],
            device_id=(d, peer), device_id_type=MESH,
        )

    images = [(iq_in, iq), (ik_in, ik), (iv_in, iv)]
    image_own = []
    for a, (src, dst) in enumerate(images):
        copy = pltpu.make_async_copy(
            columns_of(src, t), dst.at[t], img_own.at[a]
        )
        copy.start()
        image_own.append(copy)
        for peer in peers:
            image_copy(a, src, dst, peer, t).start()

    for copy in own[2:]:
        copy.wait()

    ccols = scale.shape[2]
    for j in range(n):
        scale[j] = scale_ref[:, j * ccols:(j + 1) * ccols]
        shift[j] = shift_ref[:, j * ccols:(j + 1) * ccols]

    slots, enc = x_ref.shape
    length = len_ref[0]

    @pl.loop(0, slots // 32)
    def _(i):
        block = pl.ds(pl.multiple_of(i * 32, 32), 32)
        x = x_ref[block, :].astype(F32)
        scale = lax.rsqrt(jnp.mean(x * x, axis=-1, keepdims=True) + EPS)
        normed[block, :] = (x * scale * gain_ref[...]).astype(BF16)

    width = q_in.shape[1]

    def project(weight, result):
        @pl.loop(0, width // 256)
        def _(j):
            block = pl.ds(pl.multiple_of(j * 256, 256), 256)
            w = weight[:, :, block].reshape(enc, 256)
            result[:, block] = jnp.dot(normed[...], w, preferred_element_type=F32).astype(BF16)

    score = functools.partial(
        lax.dot_general, dimension_numbers=(((1,), (1,)), ((), ())), preferred_element_type=F32
    )

    def head(h):
        return slice(h * HEAD, (h + 1) * HEAD)

    def await_images():
        for a, (src, dst) in enumerate(images):
            image_own[a].wait()
            for peer in peers:
                image_copy(a, src, dst, peer, peer).wait_recv()

    def image_head(h):
        keys = ik[:, :, head(h)].reshape(nt * lat, HEAD)
        values = iv[:, :, head(h)].reshape(nt * lat, HEAD)
        queries = iq[:, :, head(h)].reshape(nt * lat, HEAD)
        scores = score(queries, keys) * HEAD ** (-0.5)
        top = jnp.max(scores, axis=-1, keepdims=True)
        expo = jnp.exp(scores - top)
        part_top[h] = top
        part_sum[h] = jnp.sum(expo, axis=-1, keepdims=True)
        part_out[h] = jnp.dot(expo.astype(BF16), values, preferred_element_type=F32)

    def encoder_head(h):
        scores = score(eq[:, head(h)], ek[:, head(h)])
        valid = lax.broadcasted_iota(jnp.int32, scores.shape, 1) < length
        scores = jnp.where(valid, scores, -jnp.inf)
        expo = jnp.exp(scores - jnp.max(scores, axis=-1, keepdims=True))
        sums[h] = jnp.sum(expo, axis=-1, keepdims=True)
        probs[h] = expo.astype(BF16)

    image_heads = cols // HEAD
    encoder_heads = width // HEAD
    tasks = [await_images] + [functools.partial(image_head, h) for h in range(image_heads)]
    run_ring(group_qk, 1, n - 1, tasks)
    tasks = tasks[n - 2:]
    open_ring(group_vo)
    close_ring(group_qk)

    def encoder_pair(h):
        for one in range(h, min(h + 2, encoder_heads)):
            encoder_head(one)

    project(wq, eq)
    tasks = [functools.partial(project, wk, ek)] + tasks
    tasks += [functools.partial(encoder_pair, h) for h in range(0, encoder_heads, 2)]
    run_ring(group_vo, 1, n - 1, tasks)
    for task in tasks[n - 2:]:
        task()
    open_ring(group_c)
    open_ring(group_t)
    close_ring(group_vo)
    project(wv, ev)
    for h in range(encoder_heads):
        value = jnp.dot(probs[h], ev[:, head(h)], preferred_element_type=F32)
        mixed[:, head(h)] = (value / sums[h]).astype(BF16)
    run_ring(group_c, 1, 2)

    ocols = o_in.shape[1]
    share = enc // nt
    per = share // ocols

    @pl.loop(0, n)
    def _(j):
        value = jnp.dot(mixed[...], wo[j], preferred_element_type=F32).astype(BF16)
        part[j // per, :, pl.ds(pl.multiple_of((j % per) * ocols, 128), ocols)] = value

    def part_copy(peer, place_of):
        return pltpu.make_async_remote_copy(
            src_ref=part.at[peer], dst_ref=part_in.at[place_of],
            send_sem=part_send.at[peer], recv_sem=part_recv.at[place_of],
            device_id=(d, peer), device_id_type=MESH,
        )

    for peer in peers:
        part_copy(peer, t).start()
    arrive = 2 + (n - 2) // 3
    run_ring(group_c, 2, arrive)
    for peer in peers:
        part_copy(peer, peer).wait_recv()

    @pl.loop(0, slots // 32)
    def _(i):
        block = pl.ds(pl.multiple_of(i * 32, 32), 32)
        total = part[t, block, :].astype(F32)
        for peer in peers:
            total = total + part_in[peer, block, :].astype(F32)
        x = x_ref[block, pl.ds(pl.multiple_of(t * share, 128), share)].astype(F32)
        emb[block, :] = (x + total).astype(BF16)

    run_ring(group_c, arrive, n - 1)
    run_ring(group_t, 1, 2)
    close_ring(group_c)

    @pl.loop(0, n)
    def _(j):
        ctx[j] = score(emb[...], wc[j]).astype(BF16)

    trow = slots // nt

    def token_rows(who):
        return pl.ds(pl.multiple_of(who * trow, 16), trow)

    def ctx_copy(peer, place_of):
        return pltpu.make_async_remote_copy(
            src_ref=ctx.at[:, token_rows(peer)], dst_ref=ctx_in.at[place_of],
            send_sem=ctx_send.at[peer], recv_sem=ctx_recv.at[place_of],
            device_id=(d, peer), device_id_type=MESH,
        )

    for peer in peers:
        ctx_copy(peer, t).start()
    middle = 2 + (n - 1) // 3
    run_ring(group_t, 2, middle)
    for peer in peers:
        ctx_copy(peer, peer).wait_recv()
    context = ctx[:, token_rows(t), :].astype(F32)
    for peer in peers:
        context = context + ctx_in[peer].astype(F32)
    features = context.shape[0] * context.shape[2]

    def mean(values):
        return jnp.sum(jnp.sum(values, axis=0), axis=-1, keepdims=True)[None] / features

    centered = context - mean(context)
    spread = mean(centered * centered)
    modulated = centered * lax.rsqrt(spread + EPS) * (1.0 + scale[...]) + shift[...]
    mod[:, token_rows(t), :] = modulated.astype(BF16)

    def mod_copy(peer, place_of):
        view = mod.at[:, token_rows(place_of)]
        return pltpu.make_async_remote_copy(
            src_ref=view, dst_ref=view,
            send_sem=mod_send.at[peer], recv_sem=mod_recv.at[place_of],
            device_id=(d, peer), device_id_type=MESH,
        )

    for peer in peers:
        mod_copy(peer, t).start()
    run_ring(group_t, middle, n - 1)
    for peer in peers:
        mod_copy(peer, peer).wait_recv()
    close_ring(group_t)

    def text_project(weight, result):
        total = jnp.dot(mod[0], weight[0], preferred_element_type=F32)
        for j in range(1, n):
            total = total + jnp.dot(mod[j], weight[j], preferred_element_type=F32)
        result[...] = total.astype(BF16)

    text_project(wtk, tk)
    text_project(wtv, tv)

    for h in range(image_heads):
        queries = iq[:, :, head(h)].reshape(nt * lat, HEAD)
        scores = score(queries, tk[:, head(h)]) * HEAD ** (-0.5)
        valid = lax.broadcasted_iota(jnp.int32, scores.shape, 1) < length
        scores = jnp.where(valid, scores, -jnp.inf)
        top = jnp.maximum(part_top[h], jnp.max(scores, axis=-1, keepdims=True))
        expo = jnp.exp(scores - top)
        shrink = jnp.exp(part_top[h] - top)
        total = part_sum[h] * shrink + jnp.sum(expo, axis=-1, keepdims=True)
        value = jnp.dot(expo.astype(BF16), tv[:, head(h)], preferred_element_type=F32)
        value = part_out[h] * shrink + value
        att[:, :, head(h)] = (value / total).astype(BF16).reshape(nt, lat, HEAD)

    def att_copy(peer, place_of):
        return pltpu.make_async_remote_copy(
            src_ref=att.at[peer], dst_ref=columns_of(out_ref, place_of),
            send_sem=att_send.at[peer], recv_sem=att_recv.at[place_of],
            device_id=(d, peer), device_id_type=MESH,
        )

    for peer in peers:
        att_copy(peer, t).start()
    copy = pltpu.make_async_copy(att.at[t], columns_of(out_ref, t), att_own)
    copy.start()
    copy.wait()
    for peer in peers:
        for a, (src, dst) in enumerate(images):
            image_copy(a, src, dst, peer, t).wait_send()
        part_copy(peer, t).wait_send()
        ctx_copy(peer, t).wait_send()
        mod_copy(peer, t).wait_send()
        att_copy(peer, t).wait_send()
    for peer in peers:
        att_copy(peer, peer).wait_recv()


def per_device(
    n, nt,
    text_states, prompt_lengths, attn_gain, query_w, key_w, value_w, out_w, context_w,
    mod_scale, mod_shift, text_key_w, text_value_w, image_query, image_key, image_value,
):
    prompts, slots, enc = text_states.shape
    lat, joint = image_query.shape[1:]
    width = query_w.shape[1]
    cols = joint // nt
    ccols = context_w.shape[1]
    vmem = pl.BlockSpec(memory_space=pltpu.VMEM)
    anywhere = pl.BlockSpec(memory_space=pl.ANY)
    dma = pltpu.SemaphoreType.DMA
    scratch = [pltpu.VMEM((n,) + w.shape, BF16) for w in (query_w, key_w, value_w, out_w, context_w.T, text_key_w, text_value_w)]
    scratch += [
        pltpu.VMEM((slots, enc), BF16),
        pltpu.VMEM((slots, width), BF16),
        pltpu.VMEM((slots, width), BF16),
        pltpu.VMEM((slots, width), BF16),
        pltpu.VMEM((slots, width), BF16),
        pltpu.VMEM((nt, slots, enc // nt), BF16),
        pltpu.VMEM((nt, slots, enc // nt), BF16),
        pltpu.VMEM((slots, enc // nt), BF16),
        pltpu.VMEM((n, slots, ccols), BF16),
        pltpu.VMEM((nt, n, slots // nt, ccols), BF16),
        pltpu.VMEM((n, slots, ccols), BF16),
        pltpu.VMEM((nt, lat, cols), BF16),
        pltpu.VMEM((nt, lat, cols), BF16),
        pltpu.VMEM((nt, lat, cols), BF16),
        pltpu.VMEM((slots, cols), BF16),
        pltpu.VMEM((slots, cols), BF16),
        pltpu.VMEM((nt, lat, cols), BF16),
        pltpu.VMEM((n, 1, ccols), F32),
        pltpu.VMEM((n, 1, ccols), F32),
        pltpu.VMEM((width // HEAD, slots, slots), BF16),
        pltpu.VMEM((width // HEAD, slots, 1), F32),
        pltpu.VMEM((cols // HEAD, nt * lat, 1), F32),
        pltpu.VMEM((cols // HEAD, nt * lat, 1), F32),
        pltpu.VMEM((cols // HEAD, nt * lat, HEAD), F32),
        dma((7,)), dma((16,)), dma((16, n - 1)),
        dma((3, nt)), dma((3, nt)), dma((3,)),
        dma((nt,)), dma((nt,)), dma((nt,)), dma((nt,)), dma((nt,)), dma((nt,)),
        dma((nt,)), dma((nt,)), dma,
    ]
    flops = 2 * slots * (enc * width * 4 + enc // nt * ccols * n + ccols * n * cols * 2) + 4 * lat * nt * (lat * nt + slots) * cols
    apart = cols % 128 != 0

    def laid_out(array):
        array = array.reshape(lat, joint)
        return array.reshape(lat, nt, cols).swapaxes(0, 1) if apart else array

    result = pl.pallas_call(
        functools.partial(kernel, n, nt),
        out_shape=jax.ShapeDtypeStruct((nt, lat, cols) if apart else (lat, joint), BF16),
        in_specs=[pl.BlockSpec(memory_space=pltpu.SMEM)] + [vmem] * 4 + [anywhere] * 10,
        out_specs=vmem,
        scratch_shapes=scratch,
        compiler_params=pltpu.CompilerParams(
            collective_id=0, has_side_effects=True, vmem_limit_bytes=60 * 2**20
        ),
        cost_estimate=pl.CostEstimate(flops=flops, bytes_accessed=12 * 2**20, transcendentals=3 * 2**20),
    )(
        prompt_lengths,
        text_states.reshape(slots, enc),
        attn_gain.reshape(1, enc),
        mod_scale,
        mod_shift,
        query_w, key_w, value_w, out_w, context_w.T, text_key_w, text_value_w,
        laid_out(image_query), laid_out(image_key), laid_out(image_value),
    )
    if apart:
        result = result.swapaxes(0, 1)
    return result.reshape(1, lat, joint)


def solution(mesh):
    n, nt = mesh.shape["dp"], mesh.shape["tensor"]
    in_specs = (
        P("dp", None, None),
        P("dp"),
        P(),
        P("dp", "tensor"),
        P("dp", "tensor"),
        P("dp", "tensor"),
        P("tensor", "dp"),
        P("tensor", "dp"),
        P("dp", None),
        P("dp", None),
        P("dp", "tensor"),
        P("dp", "tensor"),
        P("dp", "tensor", None),
        P("dp", "tensor", None),
        P("dp", "tensor", None),
    )
    return jax.shard_map(
        functools.partial(per_device, n, nt),
        mesh=mesh, in_specs=in_specs, out_specs=P("dp", "tensor", None), check_vma=False,
    )
```

```python
import functools

import jax
import jax.numpy as jnp
from jax import lax
from jax.experimental import pallas as pl
from jax.experimental.pallas import tpu as pltpu
from jax.sharding import PartitionSpec as P

HEAD = 64
EPS = 1e-06
MESH = pl.DeviceIdType.MESH
F32 = jnp.float32
BF16 = jnp.bfloat16


def split_rows(rows, count):
    if rows % 16:
        return [(0, rows)]
    size = -(-rows // (count * 16)) * 16
    return [(i * size, min(size, rows - i * size)) for i in range(count)]


def kernel(n, nt, *refs):
    (
        len_ref, x_ref, gain_ref, scale_ref, shift_ref,
        q_in, k_in, v_in, o_in, c_in, tk_in, tv_in, iq_in, ik_in, iv_in,
        out_ref,
        wq, wk, wv, wo, wc, wtk, wtv,
        normed, eq, ek, ev, mixed, part, part_in, emb, ctx, ctx_in, mod,
        iq, ik, iv, tk, tv, att, scale, shift, probs, sums, part_top, part_sum, part_out,
        own_sem, ring_send, ring_recv, img_send, img_recv, img_own,
        part_send, part_recv, ctx_send, ctx_recv, mod_send, mod_recv,
        att_send, att_recv, att_own,
    ) = refs
    d = lax.axis_index("dp")
    t = lax.axis_index("tensor")
    half = n // 2

    def device_at(place):
        back = place // half
        return 2 * (place * (1 - back) + (n - 1 - place) * back) + back

    odd = d % 2
    place = (d // 2) * (1 - odd) + (n - 1 - d // 2) * odd
    right = device_at((place + 1) % n)
    left = device_at((place + n - 1) % n)
    peers = [(t + k) % nt for k in range(1, nt)]

    barrier = pltpu.get_barrier_semaphore()
    for neighbour in (left, right):
        pl.semaphore_signal(barrier, inc=1, device_id=(neighbour, t), device_id_type=MESH)
    for peer in peers:
        pl.semaphore_signal(barrier, inc=1, device_id=(d, peer), device_id_type=MESH)

    weights = [(q_in, wq), (k_in, wk), (v_in, wv), (o_in, wo), (c_in, wc), (tk_in, wtk), (tv_in, wtv)]
    own = [
        pltpu.make_async_copy(src, dst.at[d], own_sem.at[i])
        for i, (src, dst) in enumerate(weights)
    ]
    for copy in own:
        copy.start()
    pl.semaphore_wait(barrier, 2 + nt - 1)

    chunks = []

    def add(weight, index, runs, forward):
        made = []
        for run in runs:
            made.append((len(chunks), weight, run, forward))
            chunks.append(made[-1])
        return made

    def hop(chunk, step, incoming=False):
        number, weight, (start, size), forward = chunk
        back = step + 1 if incoming else step
        owner = device_at((place - back + n) % n if forward else (place + back) % n)
        view = weight.at[owner, pl.ds(start, size)] if size < weight.shape[1] else weight.at[owner]
        return pltpu.make_async_remote_copy(
            src_ref=view, dst_ref=view,
            send_sem=ring_send.at[number], recv_sem=ring_recv.at[number, step],
            device_id=(right if forward else left, t), device_id_type=MESH,
        )

    def open_ring(group):
        for chunk in group:
            hop(chunk, 0).start()

    def move(group, step):
        for chunk in group:
            hop(chunk, step - 1, incoming=True).wait_recv()
            hop(chunk, step - 1).wait_send()
            hop(chunk, step).start()

    def run_ring(group, first, last):
        @pl.loop(first, last)
        def _(step):
            move(group, step)

    def close_ring(group):
        for chunk in group:
            hop(chunk, n - 2, incoming=True).wait_recv()
            hop(chunk, n - 2).wait_send()

    rows = q_in.shape[0]
    group_qk = add(wq, 0, split_rows(rows, 2), True) + add(wk, 1, split_rows(rows, 2), False)
    group_vo = add(wv, 2, split_rows(rows, 2), True) + add(wo, 3, split_rows(o_in.shape[0], 2), False)
    quarters = split_rows(c_in.shape[0], 4)
    group_c = add(wc, 4, quarters[:2], True) + add(wc, 4, quarters[2:], False)
    trows = tk_in.shape[0]
    group_t = add(wtk, 5, split_rows(trows, 2), True) + add(wtv, 6, split_rows(trows, 2), False)

    own[0].wait()
    own[1].wait()
    open_ring(group_qk)

    lat, cols = iq.shape[1:]

    def columns_of(ref, who):
        if len(ref.shape) == 3:
            return ref.at[who]
        return ref.at[:, pl.ds(pl.multiple_of(who * cols, 128), cols)]

    def image_copy(a, src, dst, peer, place_of):
        return pltpu.make_async_remote_copy(
            src_ref=columns_of(src, peer),
            dst_ref=dst.at[place_of],
            send_sem=img_send.at[a, peer], recv_sem=img_recv.at[a, place_of],
            device_id=(d, peer), device_id_type=MESH,
        )

    images = [(iq_in, iq), (ik_in, ik), (iv_in, iv)]
    image_own = []
    for a, (src, dst) in enumerate(images):
        copy = pltpu.make_async_copy(
            columns_of(src, t), dst.at[t], img_own.at[a]
        )
        copy.start()
        image_own.append(copy)
        for peer in peers:
            image_copy(a, src, dst, peer, t).start()

    for copy in own[2:]:
        copy.wait()

    ccols = scale.shape[2]
    for j in range(n):
        scale[j] = scale_ref[:, j * ccols:(j + 1) * ccols]
        shift[j] = shift_ref[:, j * ccols:(j + 1) * ccols]

    slots, enc = x_ref.shape
    length = len_ref[0]

    @pl.loop(0, slots // 32)
    def _(i):
        block = pl.ds(pl.multiple_of(i * 32, 32), 32)
        x = x_ref[block, :].astype(F32)
        scale = lax.rsqrt(jnp.mean(x * x, axis=-1, keepdims=True) + EPS)
        normed[block, :] = (x * scale * gain_ref[...]).astype(BF16)

    width = q_in.shape[1]

    def project(weight, result):
        @pl.loop(0, width // 256)
        def _(j):
            block = pl.ds(pl.multiple_of(j * 256, 256), 256)
            w = weight[:, :, block].reshape(enc, 256)
            result[:, block] = jnp.dot(normed[...], w, preferred_element_type=F32).astype(BF16)

    score = functools.partial(
        lax.dot_general, dimension_numbers=(((1,), (1,)), ((), ())), preferred_element_type=F32
    )

    def head(h):
        return slice(h * HEAD, (h + 1) * HEAD)

    def await_images():
        for a, (src, dst) in enumerate(images):
            image_own[a].wait()
            for peer in peers:
                image_copy(a, src, dst, peer, peer).wait_recv()

    def image_head(h):
        keys = ik[:, :, head(h)].reshape(nt * lat, HEAD)
        values = iv[:, :, head(h)].reshape(nt * lat, HEAD)
        queries = iq[:, :, head(h)].reshape(nt * lat, HEAD)
        scores = score(queries, keys) * HEAD ** (-0.5)
        top = jnp.max(scores, axis=-1, keepdims=True)
        expo = jnp.exp(scores - top)
        part_top[h] = top
        part_sum[h] = jnp.sum(expo, axis=-1, keepdims=True)
        part_out[h] = jnp.dot(expo.astype(BF16), values, preferred_element_type=F32)

    def encoder_head(h):
        scores = score(eq[:, head(h)], ek[:, head(h)])
        valid = lax.broadcasted_iota(jnp.int32, scores.shape, 1) < length
        scores = jnp.where(valid, scores, -jnp.inf)
        expo = jnp.exp(scores - jnp.max(scores, axis=-1, keepdims=True))
        sums[h] = jnp.sum(expo, axis=-1, keepdims=True)
        probs[h] = expo.astype(BF16)

    image_heads = cols // HEAD
    encoder_heads = width // HEAD
    def encoder_run(first, last):
        for h in range(first, last):
            encoder_head(h)

    tasks = [await_images] + [functools.partial(image_head, h) for h in range(image_heads)]
    lag = 2
    move(group_qk, 1)
    move(group_qk, 2)
    open_ring(group_vo)
    for step in range(3, min(n - 1, 7)):
        move(group_qk, step)
        for task in tasks[:1]:
            task()
        move(group_vo, step - lag)
        for task in tasks[1:2]:
            task()
        tasks = tasks[2:]
    if n - 1 > 7:
        @pl.loop(7, n - 1)
        def _(step):
            move(group_qk, step)
            move(group_vo, step - lag)
    for task in tasks:
        task()
    close_ring(group_qk)
    project(wq, eq)
    move(group_vo, n - 3)
    project(wk, ek)
    encoder_run(0, encoder_heads // 2)
    move(group_vo, n - 2)
    open_ring(group_c)
    open_ring(group_t)
    encoder_run(encoder_heads // 2, encoder_heads)
    close_ring(group_vo)
    project(wv, ev)
    for h in range(encoder_heads):
        value = jnp.dot(probs[h], ev[:, head(h)], preferred_element_type=F32)
        mixed[:, head(h)] = (value / sums[h]).astype(BF16)
    run_ring(group_c, 1, 2)

    ocols = o_in.shape[1]
    share = enc // nt
    per = share // ocols

    @pl.loop(0, n)
    def _(j):
        value = jnp.dot(mixed[...], wo[j], preferred_element_type=F32).astype(BF16)
        part[j // per, :, pl.ds(pl.multiple_of((j % per) * ocols, 128), ocols)] = value

    def part_copy(peer, place_of):
        return pltpu.make_async_remote_copy(
            src_ref=part.at[peer], dst_ref=part_in.at[place_of],
            send_sem=part_send.at[peer], recv_sem=part_recv.at[place_of],
            device_id=(d, peer), device_id_type=MESH,
        )

    for peer in peers:
        part_copy(peer, t).start()
    arrive = 3 + (n - 2) // 3
    run_ring(group_c, 2, arrive)
    for peer in peers:
        part_copy(peer, peer).wait_recv()

    @pl.loop(0, slots // 32)
    def _(i):
        block = pl.ds(pl.multiple_of(i * 32, 32), 32)
        total = part[t, block, :].astype(F32)
        for peer in peers:
            total = total + part_in[peer, block, :].astype(F32)
        x = x_ref[block, pl.ds(pl.multiple_of(t * share, 128), share)].astype(F32)
        emb[block, :] = (x + total).astype(BF16)

    run_ring(group_c, arrive, n - 1)
    run_ring(group_t, 1, 2)
    close_ring(group_c)

    @pl.loop(0, n)
    def _(j):
        ctx[j] = score(emb[...], wc[j]).astype(BF16)

    trow = slots // nt

    def token_rows(who):
        return pl.ds(pl.multiple_of(who * trow, 16), trow)

    def ctx_copy(peer, place_of):
        return pltpu.make_async_remote_copy(
            src_ref=ctx.at[:, token_rows(peer)], dst_ref=ctx_in.at[place_of],
            send_sem=ctx_send.at[peer], recv_sem=ctx_recv.at[place_of],
            device_id=(d, peer), device_id_type=MESH,
        )

    for peer in peers:
        ctx_copy(peer, t).start()
    middle = 3 + (n - 1) // 3
    run_ring(group_t, 2, middle)
    for peer in peers:
        ctx_copy(peer, peer).wait_recv()
    context = ctx[:, token_rows(t), :].astype(F32)
    for peer in peers:
        context = context + ctx_in[peer].astype(F32)
    features = context.shape[0] * context.shape[2]

    def mean(values):
        return jnp.sum(jnp.sum(values, axis=0), axis=-1, keepdims=True)[None] / features

    centered = context - mean(context)
    spread = mean(centered * centered)
    modulated = centered * lax.rsqrt(spread + EPS) * (1.0 + scale[...]) + shift[...]
    mod[:, token_rows(t), :] = modulated.astype(BF16)

    def mod_copy(peer, place_of):
        view = mod.at[:, token_rows(place_of)]
        return pltpu.make_async_remote_copy(
            src_ref=view, dst_ref=view,
            send_sem=mod_send.at[peer], recv_sem=mod_recv.at[place_of],
            device_id=(d, peer), device_id_type=MESH,
        )

    for peer in peers:
        mod_copy(peer, t).start()
    run_ring(group_t, middle, n - 1)
    for peer in peers:
        mod_copy(peer, peer).wait_recv()
    close_ring(group_t)

    def text_project(weight, result):
        total = jnp.dot(mod[0], weight[0], preferred_element_type=F32)
        for j in range(1, n):
            total = total + jnp.dot(mod[j], weight[j], preferred_element_type=F32)
        result[...] = total.astype(BF16)

    text_project(wtk, tk)
    text_project(wtv, tv)

    for h in range(image_heads):
        queries = iq[:, :, head(h)].reshape(nt * lat, HEAD)
        scores = score(queries, tk[:, head(h)]) * HEAD ** (-0.5)
        valid = lax.broadcasted_iota(jnp.int32, scores.shape, 1) < length
        scores = jnp.where(valid, scores, -jnp.inf)
        top = jnp.maximum(part_top[h], jnp.max(scores, axis=-1, keepdims=True))
        expo = jnp.exp(scores - top)
        shrink = jnp.exp(part_top[h] - top)
        total = part_sum[h] * shrink + jnp.sum(expo, axis=-1, keepdims=True)
        value = jnp.dot(expo.astype(BF16), tv[:, head(h)], preferred_element_type=F32)
        value = part_out[h] * shrink + value
        att[:, :, head(h)] = (value / total).astype(BF16).reshape(nt, lat, HEAD)

    def att_copy(peer, place_of):
        return pltpu.make_async_remote_copy(
            src_ref=att.at[peer], dst_ref=columns_of(out_ref, place_of),
            send_sem=att_send.at[peer], recv_sem=att_recv.at[place_of],
            device_id=(d, peer), device_id_type=MESH,
        )

    for peer in peers:
        att_copy(peer, t).start()
    copy = pltpu.make_async_copy(att.at[t], columns_of(out_ref, t), att_own)
    copy.start()
    copy.wait()
    for peer in peers:
        for a, (src, dst) in enumerate(images):
            image_copy(a, src, dst, peer, t).wait_send()
        part_copy(peer, t).wait_send()
        ctx_copy(peer, t).wait_send()
        mod_copy(peer, t).wait_send()
        att_copy(peer, t).wait_send()
    for peer in peers:
        att_copy(peer, peer).wait_recv()


def per_device(
    n, nt,
    text_states, prompt_lengths, attn_gain, query_w, key_w, value_w, out_w, context_w,
    mod_scale, mod_shift, text_key_w, text_value_w, image_query, image_key, image_value,
):
    prompts, slots, enc = text_states.shape
    lat, joint = image_query.shape[1:]
    width = query_w.shape[1]
    cols = joint // nt
    ccols = context_w.shape[1]
    vmem = pl.BlockSpec(memory_space=pltpu.VMEM)
    anywhere = pl.BlockSpec(memory_space=pl.ANY)
    dma = pltpu.SemaphoreType.DMA
    scratch = [pltpu.VMEM((n,) + w.shape, BF16) for w in (query_w, key_w, value_w, out_w, context_w.T, text_key_w, text_value_w)]
    scratch += [
        pltpu.VMEM((slots, enc), BF16),
        pltpu.VMEM((slots, width), BF16),
        pltpu.VMEM((slots, width), BF16),
        pltpu.VMEM((slots, width), BF16),
        pltpu.VMEM((slots, width), BF16),
        pltpu.VMEM((nt, slots, enc // nt), BF16),
        pltpu.VMEM((nt, slots, enc // nt), BF16),
        pltpu.VMEM((slots, enc // nt), BF16),
        pltpu.VMEM((n, slots, ccols), BF16),
        pltpu.VMEM((nt, n, slots // nt, ccols), BF16),
        pltpu.VMEM((n, slots, ccols), BF16),
        pltpu.VMEM((nt, lat, cols), BF16),
        pltpu.VMEM((nt, lat, cols), BF16),
        pltpu.VMEM((nt, lat, cols), BF16),
        pltpu.VMEM((slots, cols), BF16),
        pltpu.VMEM((slots, cols), BF16),
        pltpu.VMEM((nt, lat, cols), BF16),
        pltpu.VMEM((n, 1, ccols), F32),
        pltpu.VMEM((n, 1, ccols), F32),
        pltpu.VMEM((width // HEAD, slots, slots), BF16),
        pltpu.VMEM((width // HEAD, slots, 1), F32),
        pltpu.VMEM((cols // HEAD, nt * lat, 1), F32),
        pltpu.VMEM((cols // HEAD, nt * lat, 1), F32),
        pltpu.VMEM((cols // HEAD, nt * lat, HEAD), F32),
        dma((7,)), dma((16,)), dma((16, n - 1)),
        dma((3, nt)), dma((3, nt)), dma((3,)),
        dma((nt,)), dma((nt,)), dma((nt,)), dma((nt,)), dma((nt,)), dma((nt,)),
        dma((nt,)), dma((nt,)), dma,
    ]
    flops = 2 * slots * (enc * width * 4 + enc // nt * ccols * n + ccols * n * cols * 2) + 4 * lat * nt * (lat * nt + slots) * cols
    apart = cols % 128 != 0

    def laid_out(array):
        array = array.reshape(lat, joint)
        return array.reshape(lat, nt, cols).swapaxes(0, 1) if apart else array

    result = pl.pallas_call(
        functools.partial(kernel, n, nt),
        out_shape=jax.ShapeDtypeStruct((nt, lat, cols) if apart else (lat, joint), BF16),
        in_specs=[pl.BlockSpec(memory_space=pltpu.SMEM)] + [vmem] * 4 + [anywhere] * 10,
        out_specs=vmem,
        scratch_shapes=scratch,
        compiler_params=pltpu.CompilerParams(
            collective_id=0, has_side_effects=True, vmem_limit_bytes=60 * 2**20
        ),
        cost_estimate=pl.CostEstimate(flops=flops, bytes_accessed=12 * 2**20, transcendentals=3 * 2**20),
    )(
        prompt_lengths,
        text_states.reshape(slots, enc),
        attn_gain.reshape(1, enc),
        mod_scale,
        mod_shift,
        query_w, key_w, value_w, out_w, context_w.T, text_key_w, text_value_w,
        laid_out(image_query), laid_out(image_key), laid_out(image_value),
    )
    if apart:
        result = result.swapaxes(0, 1)
    return result.reshape(1, lat, joint)


def solution(mesh):
    n, nt = mesh.shape["dp"], mesh.shape["tensor"]
    in_specs = (
        P("dp", None, None),
        P("dp"),
        P(),
        P("dp", "tensor"),
        P("dp", "tensor"),
        P("dp", "tensor"),
        P("tensor", "dp"),
        P("tensor", "dp"),
        P("dp", None),
        P("dp", None),
        P("dp", "tensor"),
        P("dp", "tensor"),
        P("dp", "tensor", None),
        P("dp", "tensor", None),
        P("dp", "tensor", None),
    )
    return jax.shard_map(
        functools.partial(per_device, n, nt),
        mesh=mesh, in_specs=in_specs, out_specs=P("dp", "tensor", None), check_vma=False,
    )
```

```python
import functools

import jax
import jax.numpy as jnp
from jax import lax
from jax.experimental import pallas as pl
from jax.experimental.pallas import tpu as pltpu
from jax.sharding import PartitionSpec as P

HEAD = 64
EPS = 1e-06
MESH = pl.DeviceIdType.MESH
F32 = jnp.float32
BF16 = jnp.bfloat16


def split_rows(rows, count):
    if rows % 16:
        return [(0, rows)]
    size = -(-rows // (count * 16)) * 16
    return [(i * size, min(size, rows - i * size)) for i in range(count)]


def kernel(n, nt, *refs):
    (
        len_ref, x_ref, gain_ref, scale_ref, shift_ref,
        q_in, k_in, v_in, o_in, c_in, tk_in, tv_in, iq_in, ik_in, iv_in,
        out_ref,
        wq, wk, wv, wo, wc, wtk, wtv,
        normed, eq, ek, ev, mixed, part, part_in, emb, ctx, ctx_in, mod,
        iq, ik, iv, tk, tv, att, scale, shift, probs, sums, part_top, part_sum, part_out,
        own_sem, ring_send, ring_recv, img_send, img_recv, img_own,
        part_send, part_recv, ctx_send, ctx_recv, mod_send, mod_recv,
        att_send, att_recv, att_own,
    ) = refs
    d = lax.axis_index("dp")
    t = lax.axis_index("tensor")
    half = n // 2

    def device_at(place):
        back = place // half
        return 2 * (place * (1 - back) + (n - 1 - place) * back) + back

    odd = d % 2
    place = (d // 2) * (1 - odd) + (n - 1 - d // 2) * odd
    right = device_at((place + 1) % n)
    left = device_at((place + n - 1) % n)
    peers = [(t + k) % nt for k in range(1, nt)]

    barrier = pltpu.get_barrier_semaphore()
    for neighbour in (left, right):
        pl.semaphore_signal(barrier, inc=1, device_id=(neighbour, t), device_id_type=MESH)
    for peer in peers:
        pl.semaphore_signal(barrier, inc=1, device_id=(d, peer), device_id_type=MESH)

    weights = [(q_in, wq), (k_in, wk), (v_in, wv), (o_in, wo), (c_in, wc), (tk_in, wtk), (tv_in, wtv)]
    own = [
        pltpu.make_async_copy(src, dst.at[d], own_sem.at[i])
        for i, (src, dst) in enumerate(weights)
    ]
    for copy in own:
        copy.start()
    pl.semaphore_wait(barrier, 2 + nt - 1)

    chunks = []

    def add(weight, index, runs, forward):
        made = []
        for run in runs:
            made.append((len(chunks), weight, run, forward))
            chunks.append(made[-1])
        return made

    def hop(chunk, step, incoming=False):
        number, weight, (start, size), forward = chunk
        back = step + 1 if incoming else step
        owner = device_at((place - back + n) % n if forward else (place + back) % n)
        view = weight.at[owner, pl.ds(start, size)] if size < weight.shape[1] else weight.at[owner]
        return pltpu.make_async_remote_copy(
            src_ref=view, dst_ref=view,
            send_sem=ring_send.at[number], recv_sem=ring_recv.at[number, step],
            device_id=(right if forward else left, t), device_id_type=MESH,
        )

    def open_ring(group):
        for chunk in group:
            hop(chunk, 0).start()

    def move(group, step):
        for chunk in group:
            hop(chunk, step - 1, incoming=True).wait_recv()
            hop(chunk, step - 1).wait_send()
            hop(chunk, step).start()

    def run_ring(group, first, last):
        @pl.loop(first, last)
        def _(step):
            move(group, step)

    def close_ring(group):
        for chunk in group:
            hop(chunk, n - 2, incoming=True).wait_recv()
            hop(chunk, n - 2).wait_send()

    rows = q_in.shape[0]
    group_qk = add(wq, 0, split_rows(rows, 2), True) + add(wk, 1, split_rows(rows, 2), False)
    group_vo = add(wv, 2, split_rows(rows, 2), True) + add(wo, 3, split_rows(o_in.shape[0], 2), False)
    quarters = split_rows(c_in.shape[0], 4)
    group_c = add(wc, 4, quarters[:2], True) + add(wc, 4, quarters[2:], False)
    trows = tk_in.shape[0]
    group_t = add(wtk, 5, split_rows(trows, 2), True) + add(wtv, 6, split_rows(trows, 2), False)

    own[0].wait()
    own[1].wait()
    open_ring(group_qk)

    lat, cols = iq.shape[1:]

    def columns_of(ref, who):
        if len(ref.shape) == 3:
            return ref.at[who]
        return ref.at[:, pl.ds(pl.multiple_of(who * cols, 128), cols)]

    def image_copy(a, src, dst, peer, place_of):
        return pltpu.make_async_remote_copy(
            src_ref=columns_of(src, peer),
            dst_ref=dst.at[place_of],
            send_sem=img_send.at[a, peer], recv_sem=img_recv.at[a, place_of],
            device_id=(d, peer), device_id_type=MESH,
        )

    images = [(iq_in, iq), (ik_in, ik), (iv_in, iv)]
    image_own = []
    for a, (src, dst) in enumerate(images):
        copy = pltpu.make_async_copy(
            columns_of(src, t), dst.at[t], img_own.at[a]
        )
        copy.start()
        image_own.append(copy)
        for peer in peers:
            image_copy(a, src, dst, peer, t).start()

    for copy in own[2:]:
        copy.wait()

    ccols = scale.shape[2]
    for j in range(n):
        scale[j] = scale_ref[:, j * ccols:(j + 1) * ccols]
        shift[j] = shift_ref[:, j * ccols:(j + 1) * ccols]

    slots, enc = x_ref.shape
    length = len_ref[0]

    @pl.loop(0, slots // 32)
    def _(i):
        block = pl.ds(pl.multiple_of(i * 32, 32), 32)
        x = x_ref[block, :].astype(F32)
        scale = lax.rsqrt(jnp.mean(x * x, axis=-1, keepdims=True) + EPS)
        normed[block, :] = (x * scale * gain_ref[...]).astype(BF16)

    width = q_in.shape[1]

    def project(weight, result):
        @pl.loop(0, width // 256)
        def _(j):
            block = pl.ds(pl.multiple_of(j * 256, 256), 256)
            w = weight[:, :, block].reshape(enc, 256)
            result[:, block] = jnp.dot(normed[...], w, preferred_element_type=F32).astype(BF16)

    score = functools.partial(
        lax.dot_general, dimension_numbers=(((1,), (1,)), ((), ())), preferred_element_type=F32
    )

    def head(h):
        return slice(h * HEAD, (h + 1) * HEAD)

    def await_images():
        for a, (src, dst) in enumerate(images):
            image_own[a].wait()
            for peer in peers:
                image_copy(a, src, dst, peer, peer).wait_recv()

    def image_head(h):
        keys = ik[:, :, head(h)].reshape(nt * lat, HEAD)
        values = iv[:, :, head(h)].reshape(nt * lat, HEAD)
        queries = iq[:, :, head(h)].reshape(nt * lat, HEAD)
        scores = score(queries, keys) * HEAD ** (-0.5)
        top = jnp.max(scores, axis=-1, keepdims=True)
        expo = jnp.exp(scores - top)
        part_top[h] = top
        part_sum[h] = jnp.sum(expo, axis=-1, keepdims=True)
        part_out[h] = jnp.dot(expo.astype(BF16), values, preferred_element_type=F32)

    def encoder_head(h):
        scores = score(eq[:, head(h)], ek[:, head(h)])
        valid = lax.broadcasted_iota(jnp.int32, scores.shape, 1) < length
        scores = jnp.where(valid, scores, -jnp.inf)
        expo = jnp.exp(scores - jnp.max(scores, axis=-1, keepdims=True))
        sums[h] = jnp.sum(expo, axis=-1, keepdims=True)
        probs[h] = expo.astype(BF16)

    image_heads = cols // HEAD
    encoder_heads = width // HEAD
    def encoder_run(first, last):
        for h in range(first, last):
            encoder_head(h)

    tasks = [await_images] + [functools.partial(image_head, h) for h in range(image_heads)]
    lag = 2
    move(group_qk, 1)
    move(group_qk, 2)
    open_ring(group_vo)
    for step in range(3, min(n - 1, 7)):
        move(group_qk, step)
        for task in tasks[:1]:
            task()
        move(group_vo, step - lag)
        for task in tasks[1:2]:
            task()
        tasks = tasks[2:]
    if n - 1 > 7:
        @pl.loop(7, n - 1)
        def _(step):
            move(group_qk, step)
            move(group_vo, step - lag)
    for task in tasks:
        task()
    close_ring(group_qk)
    project(wq, eq)
    move(group_vo, n - 3)
    project(wk, ek)
    encoder_run(0, encoder_heads // 2)
    move(group_vo, n - 2)
    open_ring(group_c)
    open_ring(group_t)
    encoder_run(encoder_heads // 2, encoder_heads)
    close_ring(group_vo)
    project(wv, ev)
    for h in range(encoder_heads):
        value = jnp.dot(probs[h], ev[:, head(h)], preferred_element_type=F32)
        mixed[:, head(h)] = (value / sums[h]).astype(BF16)
    run_ring(group_c, 1, 2)

    ocols = o_in.shape[1]
    share = enc // nt
    per = share // ocols

    @pl.loop(0, n)
    def _(j):
        value = jnp.dot(mixed[...], wo[j], preferred_element_type=F32).astype(BF16)
        part[j // per, :, pl.ds(pl.multiple_of((j % per) * ocols, 128), ocols)] = value

    def part_copy(peer, place_of):
        return pltpu.make_async_remote_copy(
            src_ref=part.at[peer], dst_ref=part_in.at[place_of],
            send_sem=part_send.at[peer], recv_sem=part_recv.at[place_of],
            device_id=(d, peer), device_id_type=MESH,
        )

    for peer in peers:
        part_copy(peer, t).start()
    arrive = 3 + (n - 2) // 3
    run_ring(group_c, 2, arrive)
    for peer in peers:
        part_copy(peer, peer).wait_recv()

    @pl.loop(0, slots // 32)
    def _(i):
        block = pl.ds(pl.multiple_of(i * 32, 32), 32)
        total = part[t, block, :].astype(F32)
        for peer in peers:
            total = total + part_in[peer, block, :].astype(F32)
        x = x_ref[block, pl.ds(pl.multiple_of(t * share, 128), share)].astype(F32)
        emb[block, :] = (x + total).astype(BF16)

    run_ring(group_c, arrive, n - 1)
    run_ring(group_t, 1, 2)
    close_ring(group_c)

    @pl.loop(0, n)
    def _(j):
        ctx[j] = score(emb[...], wc[j]).astype(BF16)

    trow = slots // nt

    def token_rows(who):
        return pl.ds(pl.multiple_of(who * trow, 16), trow)

    def ctx_copy(peer, place_of):
        return pltpu.make_async_remote_copy(
            src_ref=ctx.at[:, token_rows(peer)], dst_ref=ctx_in.at[place_of],
            send_sem=ctx_send.at[peer], recv_sem=ctx_recv.at[place_of],
            device_id=(d, peer), device_id_type=MESH,
        )

    for peer in peers:
        ctx_copy(peer, t).start()
    middle = 3 + (n - 1) // 3
    run_ring(group_t, 2, middle)
    for peer in peers:
        ctx_copy(peer, peer).wait_recv()
    context = ctx[:, token_rows(t), :].astype(F32)
    for peer in peers:
        context = context + ctx_in[peer].astype(F32)
    features = context.shape[0] * context.shape[2]

    def mean(values):
        return jnp.sum(jnp.sum(values, axis=0), axis=-1, keepdims=True)[None] / features

    centered = context - mean(context)
    spread = mean(centered * centered)
    modulated = centered * lax.rsqrt(spread + EPS) * (1.0 + scale[...]) + shift[...]
    mod[:, token_rows(t), :] = modulated.astype(BF16)

    def mod_copy(peer, place_of):
        view = mod.at[:, token_rows(place_of)]
        return pltpu.make_async_remote_copy(
            src_ref=view, dst_ref=view,
            send_sem=mod_send.at[peer], recv_sem=mod_recv.at[place_of],
            device_id=(d, peer), device_id_type=MESH,
        )

    for peer in peers:
        mod_copy(peer, t).start()
    run_ring(group_t, middle, n - 1)
    for peer in peers:
        mod_copy(peer, peer).wait_recv()
    close_ring(group_t)

    def text_project(weight, result):
        total = jnp.dot(mod[0], weight[0], preferred_element_type=F32)
        for j in range(1, n):
            total = total + jnp.dot(mod[j], weight[j], preferred_element_type=F32)
        result[...] = total.astype(BF16)

    text_project(wtk, tk)
    text_project(wtv, tv)

    def att_copy(peer, place_of):
        return pltpu.make_async_remote_copy(
            src_ref=att.at[peer], dst_ref=columns_of(out_ref, place_of),
            send_sem=att_send.at[peer], recv_sem=att_recv.at[place_of],
            device_id=(d, peer), device_id_type=MESH,
        )

    for who in peers + [t]:
        block = pl.ds(pl.multiple_of(who * lat, 16), lat)
        for h in range(image_heads):
            scores = score(iq[who, :, head(h)], tk[:, head(h)]) * HEAD ** (-0.5)
            valid = lax.broadcasted_iota(jnp.int32, scores.shape, 1) < length
            scores = jnp.where(valid, scores, -jnp.inf)
            before = part_top[h, block, :]
            top = jnp.maximum(before, jnp.max(scores, axis=-1, keepdims=True))
            expo = jnp.exp(scores - top)
            shrink = jnp.exp(before - top)
            total = part_sum[h, block, :] * shrink + jnp.sum(expo, axis=-1, keepdims=True)
            value = jnp.dot(expo.astype(BF16), tv[:, head(h)], preferred_element_type=F32)
            value = part_out[h, block, :] * shrink + value
            att[who, :, head(h)] = (value / total).astype(BF16)
        if who is not t:
            att_copy(who, t).start()
    copy = pltpu.make_async_copy(att.at[t], columns_of(out_ref, t), att_own)
    copy.start()
    copy.wait()
    for peer in peers:
        for a, (src, dst) in enumerate(images):
            image_copy(a, src, dst, peer, t).wait_send()
        part_copy(peer, t).wait_send()
        ctx_copy(peer, t).wait_send()
        mod_copy(peer, t).wait_send()
        att_copy(peer, t).wait_send()
    for peer in peers:
        att_copy(peer, peer).wait_recv()


def per_device(
    n, nt,
    text_states, prompt_lengths, attn_gain, query_w, key_w, value_w, out_w, context_w,
    mod_scale, mod_shift, text_key_w, text_value_w, image_query, image_key, image_value,
):
    prompts, slots, enc = text_states.shape
    lat, joint = image_query.shape[1:]
    width = query_w.shape[1]
    cols = joint // nt
    ccols = context_w.shape[1]
    vmem = pl.BlockSpec(memory_space=pltpu.VMEM)
    anywhere = pl.BlockSpec(memory_space=pl.ANY)
    dma = pltpu.SemaphoreType.DMA
    scratch = [pltpu.VMEM((n,) + w.shape, BF16) for w in (query_w, key_w, value_w, out_w, context_w.T, text_key_w, text_value_w)]
    scratch += [
        pltpu.VMEM((slots, enc), BF16),
        pltpu.VMEM((slots, width), BF16),
        pltpu.VMEM((slots, width), BF16),
        pltpu.VMEM((slots, width), BF16),
        pltpu.VMEM((slots, width), BF16),
        pltpu.VMEM((nt, slots, enc // nt), BF16),
        pltpu.VMEM((nt, slots, enc // nt), BF16),
        pltpu.VMEM((slots, enc // nt), BF16),
        pltpu.VMEM((n, slots, ccols), BF16),
        pltpu.VMEM((nt, n, slots // nt, ccols), BF16),
        pltpu.VMEM((n, slots, ccols), BF16),
        pltpu.VMEM((nt, lat, cols), BF16),
        pltpu.VMEM((nt, lat, cols), BF16),
        pltpu.VMEM((nt, lat, cols), BF16),
        pltpu.VMEM((slots, cols), BF16),
        pltpu.VMEM((slots, cols), BF16),
        pltpu.VMEM((nt, lat, cols), BF16),
        pltpu.VMEM((n, 1, ccols), F32),
        pltpu.VMEM((n, 1, ccols), F32),
        pltpu.VMEM((width // HEAD, slots, slots), BF16),
        pltpu.VMEM((width // HEAD, slots, 1), F32),
        pltpu.VMEM((cols // HEAD, nt * lat, 1), F32),
        pltpu.VMEM((cols // HEAD, nt * lat, 1), F32),
        pltpu.VMEM((cols // HEAD, nt * lat, HEAD), F32),
        dma((7,)), dma((16,)), dma((16, n - 1)),
        dma((3, nt)), dma((3, nt)), dma((3,)),
        dma((nt,)), dma((nt,)), dma((nt,)), dma((nt,)), dma((nt,)), dma((nt,)),
        dma((nt,)), dma((nt,)), dma,
    ]
    flops = 2 * slots * (enc * width * 4 + enc // nt * ccols * n + ccols * n * cols * 2) + 4 * lat * nt * (lat * nt + slots) * cols
    apart = cols % 128 != 0

    def laid_out(array):
        array = array.reshape(lat, joint)
        return array.reshape(lat, nt, cols).swapaxes(0, 1) if apart else array

    result = pl.pallas_call(
        functools.partial(kernel, n, nt),
        out_shape=jax.ShapeDtypeStruct((nt, lat, cols) if apart else (lat, joint), BF16),
        in_specs=[pl.BlockSpec(memory_space=pltpu.SMEM)] + [vmem] * 4 + [anywhere] * 10,
        out_specs=vmem,
        scratch_shapes=scratch,
        compiler_params=pltpu.CompilerParams(
            collective_id=0, has_side_effects=True, vmem_limit_bytes=60 * 2**20
        ),
        cost_estimate=pl.CostEstimate(flops=flops, bytes_accessed=12 * 2**20, transcendentals=3 * 2**20),
    )(
        prompt_lengths,
        text_states.reshape(slots, enc),
        attn_gain.reshape(1, enc),
        mod_scale,
        mod_shift,
        query_w, key_w, value_w, out_w, context_w.T, text_key_w, text_value_w,
        laid_out(image_query), laid_out(image_key), laid_out(image_value),
    )
    if apart:
        result = result.swapaxes(0, 1)
    return result.reshape(1, lat, joint)


def solution(mesh):
    n, nt = mesh.shape["dp"], mesh.shape["tensor"]
    in_specs = (
        P("dp", None, None),
        P("dp"),
        P(),
        P("dp", "tensor"),
        P("dp", "tensor"),
        P("dp", "tensor"),
        P("tensor", "dp"),
        P("tensor", "dp"),
        P("dp", None),
        P("dp", None),
        P("dp", "tensor"),
        P("dp", "tensor"),
        P("dp", "tensor", None),
        P("dp", "tensor", None),
        P("dp", "tensor", None),
    )
    return jax.shard_map(
        functools.partial(per_device, n, nt),
        mesh=mesh, in_specs=in_specs, out_specs=P("dp", "tensor", None), check_vma=False,
    )
```
